128 devices in a mesh: slab: 32 (over x, z, core), coil: 4 (over y).
Axes of the slice: x: 4, y: 4, z: 4, core: 2. Of those that a mesh axis runs over, the one named last changes fastest.
Arguments:
- image_now: float32 [2, 2, 160, 25600], P(None, None, 'slab'), may hold values from -3 to 3
- coil_maps: bfloat16 [8, 2, 160, 25600], P('coil', None, 'slab'), may hold values from -3 to 3
- kspace: float32 [8, 2, 65536, 128], P('coil', None, 'slab'), may hold values from -6 to 6
- row_offset: float32 [2, 4194304], P(None, 'slab'), may hold values from 0 to 3
- col_offset: float32 [2, 4194304], P(None, 'slab'), may hold values from 0 to 31
- tile_index: int32 [2, 65536], P(None, 'slab'), may hold values from 0 to 7999
- block_fill: int32 [2, 65536], P(None, 'slab'), may hold values from 1 to 64, as said below
- slab_blocks: int32 [2, 32], P(None, 'slab'), may hold values from 1 to 2048, as said below
Outputs:
- image_next: float32 [2, 2, 160, 25600], P(None, None, 'slab')
The draws below stay inside these ranges and needn't reach their ends.
Inputs may be any that keep to these rules, and one draw needn't show every extreme that they name: Block slots b of slab q with b % 2048 >= slab_blocks[s, q] are not used, whatever kspace and the offsets hold there; for every state some slab uses all 2048 slots. The first block_fill samples of a block are used; the others are ignored, whatever kspace and the offsets hold there.
All inputs are finite; a program needn't handle non-finite values.
Results may differ from the reference program's by a relative error of at most 0.0048.
Values may be sent and summed in bfloat16 or wider, within the bound.
No kernel may reach another device: no remote copies, remote signals or barrier semaphores. Data moves between devices by JAX's collectives and lax.ppermute only.
A program may use at most 512 MiB of HBM per device.

```python
import math
import jax
import jax.numpy as jnp
from jax import lax

IMG = 160
GRID = 320
TX = 4
TY = 32
BLK = 64
STATES = 2
CAP = 2048
COILS = 8
NBLK = 65536
TILES_DEV = 8000
N_SLAB = 32


def draw_block_fill(key, part):
    short_fill = jax.random.randint(jax.random.fold_in(key, 11), (STATES, NBLK), 1, BLK)
    picker = jax.random.randint(jax.random.fold_in(key, 12), (STATES, NBLK), 0, 4)
    return jnp.where(picker == 0, short_fill, BLK).astype(jnp.int32)


def draw_slab_blocks(key, part):
    slab_ids = jnp.arange(N_SLAB, dtype=jnp.int32)
    distance = jnp.abs(2 * slab_ids + 1 - N_SLAB)
    base_load = CAP * (N_SLAB - distance) ** 2 // (N_SLAB - 1) ** 2
    raw_cut = jax.random.randint(jax.random.fold_in(key, 21), (STATES, N_SLAB), 0, 1 << 20)
    cut_load = raw_cut % (base_load[None, :] // 4 + 1)
    counts = jnp.where(distance[None, :] == 1, CAP, base_load[None, :] - cut_load)
    return jnp.maximum(counts, 1).astype(jnp.int32)


def set_ends(values, rng, least, largest):
    index_at = [jax.random.randint(jax.random.fold_in(rng, axis), (), 0, length) for axis, length in enumerate(values.shape)]
    longest = values.shape.index(max(values.shape))
    neighbour = index_at[:longest] + [(index_at[longest] + 1) % values.shape[longest]] + index_at[longest + 1:]
    return values.at[tuple(index_at)].set(least).at[tuple(neighbour)].set(largest)


def steps_of(rng, extent, pieces, least, top_value):
    loudness = 1.0
    for dim, shards_of in pieces:
        heights = jax.random.uniform(jax.random.fold_in(jax.random.fold_in(rng, 6), dim), (shards_of,), jnp.float32, least / len(pieces), top_value / len(pieces))
        loudness = loudness * jnp.repeat(jnp.exp(heights), extent[dim] // shards_of).reshape((-1,) + (1,) * (len(extent) - 1 - dim))
    return loudness


def gaussian(key, extent, deviation, reach, pieces=(), held_as=jnp.bfloat16):
    values = jax.random.normal(key, extent, jnp.float32) * deviation
    if len(pieces) > 0:
        values = steps_of(key, extent, pieces, -0.22, 0.18) * values
    return jnp.clip(values, min=-reach, max=reach).astype(held_as)


def setup_inputs(seed: int = 0) -> dict:
    streams_of = jax.random.split(jax.random.key(seed), 9)
    return {
        "image_now": gaussian(streams_of[0], (STATES, 2, IMG, IMG * IMG), 0.5, 3.0, ((2, 32),), jnp.float32),
        "coil_maps": gaussian(streams_of[1], (COILS, 2, IMG, IMG * IMG), 0.5, 3.0, ((0, 4), (2, 32))),
        "kspace": gaussian(streams_of[2], (COILS, STATES, NBLK, 2 * BLK), 1.0, 6.0, ((0, 4), (2, 32)), jnp.float32),
        "row_offset": jnp.clip(3.0 * jax.random.uniform(streams_of[3], (STATES, NBLK * BLK), jnp.float32) ** steps_of(streams_of[3], (STATES, NBLK * BLK), ((1, 32),), -0.2, 0.2), 0.0, 3.0),
        "col_offset": jnp.clip(31.0 * jax.random.uniform(streams_of[4], (STATES, NBLK * BLK), jnp.float32) ** steps_of(streams_of[4], (STATES, NBLK * BLK), ((1, 32),), -0.2, 0.2), 0.0, 31.0),
        "tile_index": set_ends(jax.random.randint(streams_of[5], (STATES, NBLK), 0, TILES_DEV), jax.random.fold_in(streams_of[5], 1), 0, TILES_DEV - 1).astype(jnp.int32),
        "block_fill": draw_block_fill(jax.random.fold_in(streams_of[8], 71), 0),
        "slab_blocks": draw_slab_blocks(jax.random.fold_in(streams_of[8], 71), 0),
    }


kernel_beta = 0.5
tv_smooth = 0.01
step_size = 0.5
tv_weight = 0.2

def dft_table(grid_len, img_len):
    freq_idx = jnp.arange(grid_len, dtype=jnp.int32) - grid_len // 2
    pos_idx = jnp.arange(img_len, dtype=jnp.int32) - img_len // 2
    phase_int = jnp.mod(freq_idx[:, None] * pos_idx[None, :], grid_len)
    angles = phase_int.astype(jnp.float32) * (2.0 * math.pi / grid_len)
    norm_scale = 1.0 / math.sqrt(grid_len)
    cosine = jnp.cos(angles) * norm_scale
    sine_part = jnp.sin(angles) * norm_scale
    from_real = jnp.stack([cosine, sine_part], axis=1)
    from_imag = jnp.stack([-sine_part, cosine], axis=1)
    return jnp.stack([from_real, from_imag], axis=0).astype(jnp.bfloat16)

def kernel_terms(samples, rows_s, cols_s, fill_s, live_s):
    slot_pos = jnp.arange(BLK, dtype=jnp.int32)
    in_use = ((slot_pos[None, :] < fill_s[:, None]) & live_s[:, None]).astype(jnp.float32)
    row_pos = jnp.arange(TX, dtype=jnp.float32)
    col_pos = jnp.arange(TY, dtype=jnp.float32)
    weight_x = jnp.exp(-kernel_beta * (row_pos[None, None, :] - rows_s[:, :, None]) ** 2)
    weight_y = jnp.exp(-kernel_beta * (col_pos[None, None, :] - cols_s[:, :, None]) ** 2)
    values = samples.reshape(samples.shape[0], samples.shape[1], 2, BLK) * in_use[None, :, None, :]
    spread = values[..., None] * weight_x[None, :, None, :, :]
    return jnp.einsum('cgrji,gjd->gcrid', spread, weight_y, precision=lax.Precision.HIGHEST)

def forward_diff(volume, along):
    length = volume.shape[along]
    later_part = lax.slice_in_dim(volume, 1, length, axis=along)
    behind = lax.slice_in_dim(volume, 0, length - 1, axis=along)
    closing = jnp.zeros_like(lax.slice_in_dim(volume, 0, 1, axis=along))
    return jnp.concatenate([later_part - behind, closing], axis=along)

def adjoint_diff(deltas, along):
    length = deltas.shape[along]
    opening = jnp.zeros_like(lax.slice_in_dim(deltas, 0, 1, axis=along))
    return jnp.concatenate([opening, lax.slice_in_dim(deltas, 0, length - 1, axis=along)], axis=along) - deltas

def normalize_flow(deltas):
    magnitude = jnp.sqrt(deltas[:, 0] ** 2 + deltas[:, 1] ** 2 + tv_smooth)
    return deltas / magnitude[:, None]

def reference(image_now, coil_maps, kspace, row_offset, col_offset, tile_index, block_fill, slab_blocks):
    image_vol = image_now.reshape(STATES, 2, IMG, IMG, IMG)
    maps_vol = coil_maps.reshape(COILS, 2, IMG, IMG, IMG)
    rows_all = row_offset.reshape(STATES, NBLK, BLK)
    cols_all = col_offset.reshape(STATES, NBLK, BLK)
    transform = dft_table(GRID, IMG)
    trans_f = transform.astype(jnp.float32)
    table_y = trans_f.reshape(2, GRID // TY, TY, 2, IMG)
    table_x = trans_f.reshape(2, GRID // TX, TX, 2, IMG)
    slot_ids = jnp.arange(NBLK, dtype=jnp.int32)
    slab_of = slot_ids // CAP
    slot_in = slot_ids % CAP
    results = []
    for state_no in range(STATES):
        live_s = slot_in < slab_blocks[state_no][slab_of]
        global_tile = (slab_of * TILES_DEV + tile_index[state_no]).astype(jnp.int32)

        def one_coil(running, coil_pair):
            samples_c, maps_c = coil_pair
            block_terms = kernel_terms(samples_c[None], rows_all[state_no], cols_all[state_no], block_fill[state_no], live_s)[:, 0]
            k_grid = jnp.zeros((N_SLAB * TILES_DEV, 2, TX, TY), jnp.float32).at[global_tile].add(block_terms)
            grid_half = k_grid.astype(jnp.bfloat16).reshape(GRID, GRID // TX, GRID // TY, 2, TX, TY)
            line_y = jnp.einsum('zabrid,rbdsm->zaism', grid_half.astype(jnp.float32), table_y).astype(jnp.bfloat16)
            line_x = jnp.einsum('zairm,raisn->znsm', line_y.astype(jnp.float32), table_x).astype(jnp.bfloat16)
            coil_image = jnp.einsum('qxrm,rqsz->zxsm', line_x.astype(jnp.float32), trans_f)
            real_part = coil_image[:, :, 0, :]
            imag_part = coil_image[:, :, 1, :]
            maps_re = maps_c[0].astype(jnp.float32)
            maps_im = maps_c[1].astype(jnp.float32)
            add_re = maps_re * real_part + maps_im * imag_part
            add_im = maps_re * imag_part - maps_im * real_part
            return (running + jnp.stack([add_re, add_im]), None)
        start_sum = jnp.zeros((2, IMG, IMG, IMG), jnp.float32)
        data_state, _ = lax.scan(one_coil, start_sum, (kspace[:, state_no], maps_vol))
        results.append(data_state)
    data_grad = jnp.stack(results)
    tv_grad = jnp.zeros_like(image_vol)
    for along in (0, 2, 3, 4):
        tv_grad = tv_grad + adjoint_diff(normalize_flow(forward_diff(image_vol, along)), along)
    result = image_vol - step_size * (data_grad + tv_weight * tv_grad)
    return result.reshape(STATES, 2, IMG, IMG * IMG)
```

```python
import math

import jax
import jax.numpy as jnp
import numpy as np
from jax import lax
from jax.experimental import pallas as pl
from jax.experimental.pallas import tpu as pltpu
from jax.sharding import PartitionSpec as P
import ml_dtypes

IMG = 160
TX = 4
TY = 32
BLK = 64
SLABS = 32

kernel_beta = 0.5
tv_smooth = 0.01
step_size = 0.5
tv_weight = 0.2

SCALE = math.sqrt(kernel_beta / math.log(2.0))
PLANES = 10
ROWS = 80
PAIRS_STEP = 8
VMEM_BYTES = 60 * 1024 * 1024


def dft_parts():
    grid_len, img_len = 2 * IMG, IMG
    freq = np.arange(grid_len) - grid_len // 2
    pos = np.arange(img_len) - img_len // 2
    angles = np.mod(freq[:, None] * pos[None, :], grid_len).astype(np.float32)
    angles = angles * np.float32(2.0 * math.pi / grid_len)
    norm = np.float32(1.0 / math.sqrt(grid_len))
    return (np.cos(angles) * norm).astype(np.float32), (np.sin(angles) * norm).astype(np.float32)


def lane_of(half, coil, m):
    j = coil * 80 + m
    return half * 128 + j if j < 128 else 256 + half * 32 + (j - 128)


def tables():
    cosine, sine = dft_parts()
    table_y = np.zeros((2, 384, 2, 384), np.float32)
    for coil in range(2):
        for half in range(2):
            for m in range(80):
                lane = lane_of(half, coil, m)
                table_y[coil, :320, 0, lane] = cosine[:, half * 80 + m]
                table_y[coil, :320, 1, lane] = sine[:, half * 80 + m]
    table_y = table_y.reshape(768, 768)
    cos_x = cosine.reshape(80, 4, 32, 5).transpose(3, 2, 0, 1)
    sin_x = sine.reshape(80, 4, 32, 5).transpose(3, 2, 0, 1)
    row_re = np.stack([cos_x, -sin_x], axis=3)
    row_im = np.stack([sin_x, cos_x], axis=3)
    table_x = np.stack([row_re, row_im]).reshape(320, 640)
    cos_z = cosine.reshape(32, 5, 2, 32, 5).transpose(4, 3, 2, 1, 0)
    sin_z = sine.reshape(32, 5, 2, 32, 5).transpose(4, 3, 2, 1, 0)
    table_z = np.stack([cos_z, sin_z]).reshape(320, 320)
    half = ml_dtypes.bfloat16
    return table_y.astype(half), table_x.astype(half), table_z.astype(half)


def grid_kernel(
    used_ref, addr_ref, fill_ref, ks_ref, row_ref, col_ref, ty_ref, tx_ref, out_ref,
    g_ref, p_ref, q_ref, s_ref,
):
    state = pl.program_id(0)
    lane = lax.broadcasted_iota(jnp.int32, (8, 128), 1)
    sub = lax.broadcasted_iota(jnp.int32, (8, 128), 0)
    left = lane < 64
    upper = sub < 4
    left_row = lax.broadcasted_iota(jnp.int32, (1, 128), 1) < 64
    col_pos = lax.broadcasted_iota(jnp.int32, (32, 128), 0).astype(jnp.float32) * SCALE
    row_pos = (sub & 3).astype(jnp.float32) * SCALE
    zero = jnp.zeros((8, 128), jnp.float32)

    def clear(i, carry):
        g_ref[pl.ds(i * 8, 8)] = jnp.zeros((8, 3, 2, 8, 128), jnp.float32)
        return carry

    lax.fori_loop(0, PLANES * ROWS // 8, clear, 0)

    def step(it, carry):
        base = it * (2 * PAIRS_STEP)
        re_rows, im_rows = [], []
        for coil in range(2):
            even = ks_ref[coil, 0, pl.ds(base, PAIRS_STEP, stride=2), :]
            odd = ks_ref[coil, 0, pl.ds(base + 1, PAIRS_STEP, stride=2), :]
            re_rows.append(jnp.where(left, even, pltpu.roll(odd, 64, 1)))
            im_rows.append(jnp.where(left, pltpu.roll(even, 64, 1), odd))
        sums, places = [], []
        for p in range(PAIRS_STEP):
            pair = it * PAIRS_STEP + p
            col_both = col_ref[pair]
            row_both = row_ref[pair]
            col = jnp.where(state == 0, col_both[0:1], col_both[1:2]) * SCALE
            row = jnp.where(state == 0, row_both[0:1], row_both[1:2]) * SCALE
            diff_y = col_pos - col
            weight_y = jnp.exp2(-(diff_y * diff_y)).astype(jnp.bfloat16)
            addr0 = addr_ref[state, base + 2 * p]
            addr1 = addr_ref[state, base + 2 * p + 1]
            spot = jnp.where(left_row, addr0 & 3, addr1 & 3)
            placed = jnp.concatenate(
                [weight_y * jnp.where(spot == b, 1.0, 0.0).astype(jnp.bfloat16) for b in range(4)],
                axis=0,
            )
            limit = jnp.where(
                left, fill_ref[state, base + 2 * p], fill_ref[state, base + 2 * p + 1] + 64
            )
            diff_x = row_pos - row
            weight_x = jnp.where(lane < limit, jnp.exp2(-(diff_x * diff_x)), 0.0)
            parts = [
                jnp.where(
                    upper,
                    jnp.broadcast_to(re_rows[coil][p : p + 1], (8, 128)),
                    jnp.broadcast_to(im_rows[coil][p : p + 1], (8, 128)),
                )
                * weight_x
                for coil in range(2)
            ]
            samples = jnp.concatenate(
                [jnp.where(left, part, zero) for part in parts]
                + [jnp.where(left, zero, part) for part in parts],
                axis=0,
            ).astype(jnp.bfloat16)
            sums.append(
                lax.dot_general(
                    samples, placed, (((1,), (1,)), ((), ())), preferred_element_type=jnp.float32
                )
            )
            places.append((addr0, addr1))
        for p in range(PAIRS_STEP):
            for which in range(2):
                addr = places[p][which]
                piece = sums[p][16 * which : 16 * which + 16].reshape(2, 8, 128)
                g_ref[addr >> 4, (addr >> 2) & 3] += piece
        return carry

    lax.fori_loop(0, (used_ref[state] + 2 * PAIRS_STEP - 1) // (2 * PAIRS_STEP), step, 0)

    def planes(pp, carry):
        tails = []
        for parity in range(2):
            plane = 2 * pp + parity
            lines = jnp.concatenate(
                [
                    g_ref[pl.ds(plane * ROWS, ROWS), quad, coil].reshape(640, 128).astype(jnp.bfloat16)
                    for coil in range(2)
                    for quad in range(3)
                ],
                axis=1,
            )
            p_ref[...] = jnp.dot(lines, ty_ref[...], preferred_element_type=jnp.float32).astype(
                jnp.bfloat16
            )
            q_ref[...] = jnp.dot(tx_ref[...], p_ref[...], preferred_element_type=jnp.float32)
            tails.append(([], []))
            for n in range(5):
                lo, hi = n * 32, 160 + n * 32
                re_part = q_ref[lo : lo + 32, 0:384] - q_ref[hi : hi + 32, 384:768]
                im_part = q_ref[hi : hi + 32, 0:384] + q_ref[lo : lo + 32, 384:768]
                for half in range(2):
                    lanes = slice(half * 128, half * 128 + 128)
                    start = (2 * parity) * 25 + n * 5
                    s_ref[half, pl.ds(start + pp, 32, stride=128), :] = re_part[:, lanes]
                    s_ref[half, pl.ds(start + 25 + pp, 32, stride=128), :] = im_part[:, lanes]
                tails[parity][0].append(re_part[:, 256:384])
                tails[parity][1].append(im_part[:, 256:384])
        lane32 = lax.broadcasted_iota(jnp.int32, (32, 128), 1)
        for n in range(5):
            pieces = [tails[0][0][n], tails[0][1][n], tails[1][0][n], tails[1][1][n]]
            for half in range(2):
                merged = None
                for place, piece in enumerate(pieces):
                    shift = (32 * (place - half)) % 128
                    moved = pltpu.roll(piece, shift, 1) if shift else piece
                    merged = (
                        moved if merged is None else jnp.where(lane32 < 32 * place, merged, moved)
                    )
                s_ref[half, pl.ds(100 + n * 5 + pp, 32, stride=128), :] = merged
        return carry

    lax.fori_loop(0, 5, planes, 0)
    for half in range(2):
        for q in range(32):
            out_ref[q, 0, half] = s_ref[half, q * 128 : q * 128 + 128, :].astype(jnp.bfloat16)


def grid_lines(used, addr, fill, kspace, rows, cols, table_y, table_x):
    return pl.pallas_call(
        grid_kernel,
        grid_spec=pltpu.PrefetchScalarGridSpec(
            num_scalar_prefetch=3,
            grid=(2,),
            in_specs=[
                pl.BlockSpec((2, 1, 2048, 128), lambda s, *_: (0, s, 0, 0)),
                pl.BlockSpec((1024, 2, 128), lambda s, *_: (0, 0, 0)),
                pl.BlockSpec((1024, 2, 128), lambda s, *_: (0, 0, 0)),
                pl.BlockSpec((768, 768), lambda s, *_: (0, 0)),
                pl.BlockSpec((320, 640), lambda s, *_: (0, 0)),
            ],
            out_specs=pl.BlockSpec((32, 1, 2, 128, 128), lambda s, *_: (0, s, 0, 0, 0)),
            scratch_shapes=[
                pltpu.VMEM((PLANES * ROWS, 3, 2, 8, 128), jnp.float32),
                pltpu.VMEM((640, 768), jnp.bfloat16),
                pltpu.VMEM((320, 768), jnp.float32),
                pltpu.VMEM((2, 32 * 128, 128), jnp.float32),
            ],
        ),
        out_shape=jax.ShapeDtypeStruct((32, 2, 2, 128, 128), jnp.bfloat16),
        compiler_params=pltpu.CompilerParams(vmem_limit_bytes=VMEM_BYTES),
        cost_estimate=pl.CostEstimate(
            flops=20_000_000_000, bytes_accessed=12_000_000, transcendentals=10_000_000
        ),
        name="grid_lines",
    )(used, addr, fill, kspace, rows, cols, table_y, table_x)


OUT_ROWS = 56


def combine_kernel(x_ref, maps_ref, tz_ref, out_ref, f_ref, t_ref):
    n = pl.program_id(0)

    @pl.when(n == 0)
    def _():
        def widen(i, carry):
            f_ref[pl.ds(i * 128, 128), :] = x_ref[i].astype(jnp.float32)
            return carry

        lax.fori_loop(0, 128, widen, 0)

    lane = lax.broadcasted_iota(jnp.int32, (160, 128), 1)
    zero = jnp.zeros((160, 128), jnp.float32)
    grad_re, grad_im, tail_re, tail_im = zero, zero, zero, zero
    for coil in range(4):

        def rows(group):
            return [
                f_ref[pl.ds(coil * 128 + group * 25 + n * 5 + pp, 32, stride=512), :]
                for pp in range(5)
            ]

        part_re = jnp.concatenate(rows(0) + rows(2), axis=0).astype(jnp.bfloat16)
        part_im = jnp.concatenate(rows(1) + rows(3), axis=0).astype(jnp.bfloat16)
        tail_rows = rows(4)
        rest = jnp.concatenate(
            tail_rows + [pltpu.roll(r, 64, 1) for r in tail_rows], axis=0
        ).astype(jnp.bfloat16)
        spread = jnp.concatenate([part_re, part_im, rest], axis=1)
        image = jnp.dot(tz_ref[...], spread, preferred_element_type=jnp.float32)
        image_re = image[:160, 0:128] - image[160:, 128:256]
        image_im = image[:160, 128:256] + image[160:, 0:128]
        map_re = maps_ref[coil, 0, 0].astype(jnp.float32)
        map_im = maps_ref[coil, 0, 1].astype(jnp.float32)
        map_tail = maps_ref[coil, 0, 2].astype(jnp.float32)
        map_swap = pltpu.roll(map_tail, 64, 1)
        grad_re = grad_re + map_re * image_re + map_im * image_im
        grad_im = grad_im + map_re * image_im - map_im * image_re
        tail_re = tail_re + image[:160, 256:] * map_tail + image[160:, 256:] * map_swap
        tail_im = tail_im + image[160:, 256:] * map_tail - image[:160, 256:] * map_swap
    for part, (grad, tail) in enumerate(((grad_re, tail_re), (grad_im, tail_im))):
        tail = tail + pltpu.roll(tail, 96, 1)
        total = grad + jnp.where(lane < 48, pltpu.roll(grad, 48, 1), pltpu.roll(tail, 48, 1))
        for z in range(5):
            t_ref[pl.ds(z * 10 + n * 2 + part, 32, stride=64), :] = total[z * 32 : z * 32 + 32]

    @pl.when(n == 4)
    def _():
        for q in range(32):
            value = t_ref[q * 64 : q * 64 + OUT_ROWS, :].astype(jnp.bfloat16)
            for copy in range(4):
                out_ref[q, copy] = value


def combine_coils(received, maps, table_z):
    return pl.pallas_call(
        combine_kernel,
        grid=(5,),
        in_specs=[
            pl.BlockSpec((128, 128, 128), lambda n: (0, 0, 0)),
            pl.BlockSpec((4, 1, 3, 160, 128), lambda n: (0, n, 0, 0, 0)),
            pl.BlockSpec((320, 320), lambda n: (0, 0)),
        ],
        out_specs=pl.BlockSpec((32, 4, OUT_ROWS, 128), lambda n: (0, 0, 0, 0)),
        out_shape=jax.ShapeDtypeStruct((32, 4, OUT_ROWS, 128), jnp.bfloat16),
        scratch_shapes=[
            pltpu.VMEM((128 * 128, 128), jnp.float32),
            pltpu.VMEM((32 * 64, 128), jnp.float32),
        ],
        compiler_params=pltpu.CompilerParams(vmem_limit_bytes=VMEM_BYTES),
        cost_estimate=pl.CostEstimate(
            flops=3_000_000_000, bytes_accessed=9_000_000, transcendentals=0
        ),
        name="combine_coils",
    )(received, maps, table_z)


def with_halo(block, sides, width):
    for axis, dim in sides:
        count = lax.axis_size(axis)
        forward = [(i, i + 1) for i in range(count - 1)]
        backward = [(target, source) for source, target in forward]
        low = lax.ppermute(
            lax.slice_in_dim(block, block.shape[dim] - width, None, axis=dim), axis, forward
        )
        high = lax.ppermute(lax.slice_in_dim(block, 0, width, axis=dim), axis, backward)
        block = jnp.concatenate([low, block, high], axis=dim)
    return block


def forward_diff(volume, along):
    length = volume.shape[along]
    later_part = lax.slice_in_dim(volume, 1, length, axis=along)
    behind = lax.slice_in_dim(volume, 0, length - 1, axis=along)
    closing = jnp.zeros_like(lax.slice_in_dim(volume, 0, 1, axis=along))
    return jnp.concatenate([later_part - behind, closing], axis=along)


def adjoint_diff(deltas, along):
    length = deltas.shape[along]
    opening = jnp.zeros_like(lax.slice_in_dim(deltas, 0, 1, axis=along))
    return (
        jnp.concatenate([opening, lax.slice_in_dim(deltas, 0, length - 1, axis=along)], axis=along)
        - deltas
    )


def normalize_flow(deltas):
    magnitude = jnp.sqrt(deltas[:, 0] ** 2 + deltas[:, 1] ** 2 + tv_smooth)
    return deltas / magnitude[:, None]


def map_pieces(coil_maps):
    maps = coil_maps.reshape(2, 2, 5, 32, 5, 2, 80)
    maps = maps.transpose(3, 5, 4, 1, 2, 0, 6).reshape(32, 2, 5, 2, 5, 160)
    main, rest = maps[..., :128], maps[..., 128:]
    rest_re, rest_im = rest[:, :, :, 0], rest[:, :, :, 1]
    tail = jnp.concatenate([rest_re, rest_im, rest_im, -rest_re], axis=-1)
    pieces = jnp.concatenate([main, tail[:, :, :, None]], axis=3)
    pieces = pieces.reshape(32, 1, 2, 75, 128)
    return jnp.broadcast_to(pieces, (32, 2, 2, 75, 128)).reshape(128, 75, 128)


def per_device(
    image_now, coil_maps, kspace, row_offset, col_offset, tile_index, block_fill, slab_blocks
):
    states = 2
    planes_img = image_now.shape[2]
    img_len = IMG
    table_y, table_x, table_z = (jnp.asarray(t) for t in tables())
    everywhere = ("slab", "coil")

    maps_sent = lax.all_to_all(map_pieces(coil_maps), everywhere, 0, 0, tiled=True)
    maps_here = maps_sent.reshape(32, 4, 5, 3, 5, 128).transpose(1, 2, 3, 4, 0, 5)
    maps_here = maps_here.reshape(4, 5, 3, 160, 128)

    slot = jnp.arange(2048, dtype=jnp.int32)
    fill = jnp.where(slot[None, :] < slab_blocks, block_fill, 0)
    addr = (tile_index // 10) * 16 + tile_index % 10
    rows = row_offset.reshape(2, 1024, 128).transpose(1, 0, 2)
    cols = col_offset.reshape(2, 1024, 128).transpose(1, 0, 2)
    lines = grid_lines(
        slab_blocks.reshape(2), addr, fill, kspace, rows, cols, table_y, table_x
    )
    received = lax.all_to_all(lines.reshape(128, 128, 128), everywhere, 0, 0, tiled=True)
    shares = combine_coils(received, maps_here, table_z)
    gathered = lax.all_to_all(
        shares.reshape(128, OUT_ROWS, 128), everywhere, 0, 0, tiled=True
    )
    grad = gathered[:, :50, :80].reshape(32, 2, 2, 5, 5, 2, 80)
    grad = grad.transpose(1, 5, 3, 0, 4, 2, 6).reshape(2, 2, planes_img, img_len * img_len)

    image_vol = image_now.reshape(states, 2, planes_img, img_len, img_len)
    padded = with_halo(image_vol.astype(jnp.bfloat16), (("slab", 2),), 1).astype(image_vol.dtype)
    first_plane = lax.axis_index("slab") * planes_img
    plane_pos = first_plane - 1 + jnp.arange(planes_img + 1, dtype=jnp.int32)
    plane_ok = ((plane_pos >= 0) & (plane_pos <= img_len - 2)).astype(jnp.float32)
    depth_delta = (padded[:, :, 1:] - padded[:, :, :-1]) * plane_ok[None, None, :, None, None]
    depth_flow = normalize_flow(depth_delta)
    tv_grad = depth_flow[:, :, :-1] - depth_flow[:, :, 1:]
    for along in (0, 3, 4):
        tv_grad = tv_grad + adjoint_diff(normalize_flow(forward_diff(image_vol, along)), along)
    base = image_vol - step_size * tv_weight * tv_grad
    base = base.reshape(states, 2, planes_img, img_len * img_len)
    return base - step_size * grad.astype(jnp.float32)


def solution(mesh):
    return jax.shard_map(
        per_device,
        mesh=mesh,
        in_specs=(
            P(None, None, "slab", None),
            P("coil", None, "slab", None),
            P("coil", None, "slab", None),
            P(None, "slab"),
            P(None, "slab"),
            P(None, "slab"),
            P(None, "slab"),
            P(None, "slab"),
        ),
        out_specs=P(None, None, "slab", None),
        check_vma=False,
    )
```

```python
import functools
import math

import jax
import jax.numpy as jnp
import numpy as np
from jax import lax
from jax.experimental import pallas as pl
from jax.experimental.pallas import tpu as pltpu
from jax.sharding import PartitionSpec as P
import ml_dtypes

IMG = 160
TX = 4
TY = 32
BLK = 64
SLABS = 32

kernel_beta = 0.5
tv_smooth = 0.01
step_size = 0.5
tv_weight = 0.2

SCALE = math.sqrt(kernel_beta / math.log(2.0))
PLANES = 10
ROWS = 80
PAIRS_STEP = 32
VMEM_BYTES = 56 * 1024 * 1024
SMALL_BYTES = 32 * 1024 * 1024


def dft_parts():
    grid_len, img_len = 2 * IMG, IMG
    freq = np.arange(grid_len) - grid_len // 2
    pos = np.arange(img_len) - img_len // 2
    angles = np.mod(freq[:, None] * pos[None, :], grid_len).astype(np.float32)
    angles = angles * np.float32(2.0 * math.pi / grid_len)
    norm = np.float32(1.0 / math.sqrt(grid_len))
    return (np.cos(angles) * norm).astype(np.float32), (np.sin(angles) * norm).astype(np.float32)


def lane_of(coil, m):
    quarter, j = m // 40, m % 40
    pair, odd = quarter // 2, quarter % 2
    if j < 32:
        return pair * 128 + coil * 64 + odd * 32 + j
    return 256 + pair * 32 + coil * 16 + odd * 8 + (j - 32)


def tables():
    cosine, sine = dft_parts()
    table_y = np.zeros((2, 384, 2, 384), np.float32)
    for coil in range(2):
        for m in range(IMG):
            lane = lane_of(coil, m)
            table_y[coil, :320, 0, lane] = cosine[:, m]
            table_y[coil, :320, 1, lane] = sine[:, m]
    table_y = table_y.reshape(768, 768)
    cos_x = cosine.reshape(80, 4, 32, 5).transpose(3, 2, 0, 1)
    sin_x = sine.reshape(80, 4, 32, 5).transpose(3, 2, 0, 1)
    row_re = np.stack([cos_x, -sin_x], axis=3)
    row_im = np.stack([sin_x, cos_x], axis=3)
    table_x = np.stack([row_re, row_im]).reshape(320, 640)
    cos_z = cosine.reshape(32, 10, 32, 5).transpose(3, 2, 1, 0)
    sin_z = sine.reshape(32, 10, 32, 5).transpose(3, 2, 1, 0)
    table_z = np.stack([cos_z, sin_z]).reshape(320, 320)
    half = ml_dtypes.bfloat16
    return table_y.astype(half), table_x.astype(half), table_z.astype(half)


def grid_kernel(
    state, used_ref, addr_ref, fill_ref, ks_ref, row_ref, col_ref, ty_ref, tx_ref, out_ref,
    g_ref, o_ref, p_ref, q_ref, s_ref, t_ref,
):
    lane = lax.broadcasted_iota(jnp.int32, (8, 128), 1)
    sub = lax.broadcasted_iota(jnp.int32, (8, 128), 0)
    left = lane < 64
    upper = sub < 4
    left_row = lax.broadcasted_iota(jnp.int32, (1, 128), 1) < 64
    col_pos = lax.broadcasted_iota(jnp.int32, (32, 128), 0).astype(jnp.float32) * SCALE
    row_pos = (sub & 3).astype(jnp.float32) * SCALE
    zero = jnp.zeros((8, 128), jnp.float32)

    def clear(i, carry):
        g_ref[pl.ds(i * 8, 8)] = jnp.zeros((8, 3, 2, 8, 128), jnp.float32)
        return carry

    lax.fori_loop(0, PLANES * ROWS // 8, clear, 0)

    def add_pair(done, p):
        first = jnp.maximum(done, 0) * (2 * PAIRS_STEP) + 2 * p
        for which in range(2):
            addr = addr_ref[state, first + which]
            g_ref[addr >> 4, (addr >> 2) & 3] += o_ref[done & 1, p, which]

    def step(it, carry):
        base = it * (2 * PAIRS_STEP)
        re_rows, im_rows = [], []
        for coil in range(2):
            even = ks_ref[coil, 0, pl.ds(base, PAIRS_STEP, stride=2), :]
            odd = ks_ref[coil, 0, pl.ds(base + 1, PAIRS_STEP, stride=2), :]
            re_rows.append(jnp.where(left_row, even, pltpu.roll(odd, 64, 1)))
            im_rows.append(jnp.where(left_row, pltpu.roll(even, 64, 1), odd))
        for p in range(PAIRS_STEP):
            add_pair(it - 1, p)
            pair = it * PAIRS_STEP + p
            col = col_ref[pair][state : state + 1] * SCALE
            row = row_ref[pair][state : state + 1] * SCALE
            diff_y = col_pos - col
            weight_y = jnp.exp2(-(diff_y * diff_y)).astype(jnp.bfloat16)
            addr0 = addr_ref[state, base + 2 * p]
            addr1 = addr_ref[state, base + 2 * p + 1]
            spot = jnp.where(left_row, addr0 & 3, addr1 & 3)
            placed = jnp.concatenate(
                [weight_y * jnp.where(spot == b, 1.0, 0.0).astype(jnp.bfloat16) for b in range(4)],
                axis=0,
            )
            limit = jnp.where(
                left, fill_ref[state, base + 2 * p], fill_ref[state, base + 2 * p + 1] + 64
            )
            diff_x = row_pos - row
            weight_x = jnp.where(lane < limit, jnp.exp2(-(diff_x * diff_x)), 0.0)
            parts = [
                jnp.where(
                    upper,
                    jnp.broadcast_to(re_rows[coil][p : p + 1], (8, 128)),
                    jnp.broadcast_to(im_rows[coil][p : p + 1], (8, 128)),
                )
                * weight_x
                for coil in range(2)
            ]
            samples = jnp.concatenate(
                [jnp.where(left, part, zero) for part in parts]
                + [jnp.where(left, zero, part) for part in parts],
                axis=0,
            ).astype(jnp.bfloat16)
            o_ref[it & 1, p] = lax.dot_general(
                samples, placed, (((1,), (1,)), ((), ())), preferred_element_type=jnp.float32
            ).reshape(2, 2, 8, 128)
        return carry

    steps = (used_ref[state] + 2 * PAIRS_STEP - 1) // (2 * PAIRS_STEP)
    o_ref[1] = jnp.zeros((PAIRS_STEP, 2, 2, 8, 128), jnp.float32)
    lax.fori_loop(0, steps, step, 0)
    for p in range(PAIRS_STEP):
        add_pair(steps - 1, p)

    lane32 = lax.broadcasted_iota(jnp.int32, (32, 128), 1)
    even32 = (lane32 // 32) % 2 == 0
    even8 = (lane32 // 8) % 2 == 0

    def one_plane(plane, carry):
        lines = jnp.concatenate(
            [
                g_ref[pl.ds(plane * ROWS, ROWS), quad, coil].reshape(640, 128).astype(jnp.bfloat16)
                for coil in range(2)
                for quad in range(3)
            ],
            axis=1,
        )
        p_ref[...] = jnp.dot(lines, ty_ref[...], preferred_element_type=jnp.float32).astype(
            jnp.bfloat16
        )
        q_ref[...] = jnp.dot(tx_ref[...], p_ref[...], preferred_element_type=jnp.float32)
        merged = [None] * 4
        for n in range(5):
            lo, hi = n * 32, 160 + n * 32
            re_part = q_ref[lo : lo + 32, 0:384] - q_ref[hi : hi + 32, 384:768]
            im_part = q_ref[hi : hi + 32, 0:384] + q_ref[lo : lo + 32, 384:768]
            for pair in range(2):
                re_e = re_part[:, pair * 128 : pair * 128 + 128]
                im_e = im_part[:, pair * 128 : pair * 128 + 128]
                at = pl.ds(n * 10 + plane, 32, stride=64)
                s_ref[2 * pair, at, :] = jnp.where(even32, re_e, pltpu.roll(im_e, 32, 1))
                s_ref[2 * pair + 1, at, :] = jnp.where(even32, pltpu.roll(re_e, 96, 1), im_e)
            re_t, im_t = re_part[:, 256:384], im_part[:, 256:384]
            rest = (
                jnp.where(even8, re_t, pltpu.roll(im_t, 8, 1)),
                jnp.where(even8, pltpu.roll(re_t, 120, 1), im_t),
            )
            if n == 4:
                for odd in range(2):
                    t_ref[plane, odd] = rest[odd]
                continue
            for quarter in range(4):
                shift = 32 * (n - quarter // 2) % 128
                moved = pltpu.roll(rest[quarter % 2], shift, 1) if shift else rest[quarter % 2]
                before = merged[quarter]
                merged[quarter] = (
                    moved if before is None else jnp.where(lane32 < 32 * n, before, moved)
                )
        for quarter in range(4):
            s_ref[quarter, pl.ds(50 + plane, 32, stride=64), :] = merged[quarter]
        return carry

    lax.fori_loop(0, PLANES, one_plane, 0)
    for quarter in range(4):
        for group in range(3):
            merged = None
            for v in range(4 if group < 2 else 2):
                shift = 32 * (v - quarter // 2) % 128
                moved = t_ref[4 * group + v, quarter % 2]
                moved = pltpu.roll(moved, shift, 1) if shift else moved
                merged = moved if merged is None else jnp.where(lane32 < 32 * v, merged, moved)
            s_ref[quarter, pl.ds(60 + group, 32, stride=64), :] = merged
        for q in range(32):
            out_ref[q, quarter] = s_ref[quarter, q * 64 : q * 64 + 64, :].astype(jnp.bfloat16)


def grid_lines(state, used, addr, fill, kspace, rows, cols, table_y, table_x):
    return pl.pallas_call(
        functools.partial(grid_kernel, state),
        grid_spec=pltpu.PrefetchScalarGridSpec(
            num_scalar_prefetch=3,
            grid=(1,),
            in_specs=[
                pl.BlockSpec((2, 1, 2048, 128), lambda i, *_: (0, state, 0, 0)),
                pl.BlockSpec((1024, 2, 128), lambda i, *_: (0, 0, 0)),
                pl.BlockSpec((1024, 2, 128), lambda i, *_: (0, 0, 0)),
                pl.BlockSpec((768, 768), lambda i, *_: (0, 0)),
                pl.BlockSpec((320, 640), lambda i, *_: (0, 0)),
            ],
            out_specs=pl.BlockSpec((32, 4, 64, 128), lambda i, *_: (0, 0, 0, 0)),
            scratch_shapes=[
                pltpu.VMEM((PLANES * ROWS, 3, 2, 8, 128), jnp.float32),
                pltpu.VMEM((2, PAIRS_STEP, 2, 2, 8, 128), jnp.float32),
                pltpu.VMEM((640, 768), jnp.bfloat16),
                pltpu.VMEM((320, 768), jnp.float32),
                pltpu.VMEM((4, 32 * 64, 128), jnp.float32),
                pltpu.VMEM((PLANES, 2, 32, 128), jnp.float32),
            ],
        ),
        out_shape=jax.ShapeDtypeStruct((32, 4, 64, 128), jnp.bfloat16),
        compiler_params=pltpu.CompilerParams(vmem_limit_bytes=VMEM_BYTES),
        cost_estimate=pl.CostEstimate(
            flops=20_000_000_000, bytes_accessed=100_000_000, transcendentals=10_000_000
        ),
        name="grid_lines",
    )(used, addr, fill, kspace, rows, cols, table_y, table_x)


def swap_parts(value, group, even):
    return jnp.where(even, pltpu.roll(value, 128 - group, 1), -pltpu.roll(value, group, 1))


def combine_kernel(state, *refs):
    if state == 0:
        x_ref, maps_ref, tz_ref, out_ref, f_ref, m_ref = refs
        t_ref = out_ref
    else:
        x_ref, maps_ref, tz_ref, before_ref, out_ref, f_ref, m_ref, t_ref = refs

    def widen(i, carry):
        f_ref[pl.ds(i * 128, 128), :] = (
            x_ref[pl.ds(2 * i, 2)].reshape(128, 128).astype(jnp.float32)
        )
        m_ref[pl.ds(i * 64, 64), :] = (
            maps_ref[pl.ds(2 * i, 2)].reshape(64, 128).astype(jnp.float32)
        )
        return carry

    lax.fori_loop(0, 64, widen, 0)

    lane = lax.broadcasted_iota(jnp.int32, (160, 128), 1)
    lane32 = lax.broadcasted_iota(jnp.int32, (32, 128), 1)
    even32 = (lane // 32) % 2 == 0
    even8 = (lane // 8) % 2 == 0
    slot8 = (lane // 8) % 4
    zero = jnp.zeros((160, 128), jnp.float32)

    def lines(coil, row):
        return f_ref[pl.ds(coil * 64 + row, 32, stride=256), :]

    def maps(coil, row):
        return m_ref[pl.ds(coil * 32 + row, 32, stride=128), :]

    def moved_to(value, source, target):
        shift = 32 * (target - source) % 128
        return pltpu.roll(value, shift, 1) if shift else value

    def summed(line_rows, map_rows, group, even):
        grad_re, grad_im = zero, zero
        for first in range(0, len(line_rows), 2):
            block = line_rows[first : first + 2]
            spread = jnp.concatenate(
                [jnp.concatenate(r, axis=0).astype(jnp.bfloat16) for r in block], axis=1
            )
            image = jnp.dot(tz_ref[...], spread, preferred_element_type=jnp.float32)
            for k in range(len(block)):
                by_cos = image[:160, k * 128 : k * 128 + 128]
                by_sin = image[160:, k * 128 : k * 128 + 128]
                here = jnp.concatenate(map_rows[first + k], axis=0)
                swapped = swap_parts(here, group, even)
                grad_re = grad_re + by_cos * here + by_sin * swapped
                grad_im = grad_im + by_sin * here - by_cos * swapped
        return grad_re, grad_im

    def put(row, value):
        t_ref[pl.ds(row, 32, stride=32), :] = value

    def over_groups(value):
        value = value + pltpu.roll(value, 64, 1)
        return value + pltpu.roll(value, 32, 1)

    def in_group(value):
        value = value + pltpu.roll(value, 112, 1)
        return value + pltpu.roll(value, 120, 1)

    def placed(grad_re, grad_im):
        moved_re = pltpu.roll(grad_re, 16, 1) if state else grad_re
        moved_im = pltpu.roll(grad_im, 16 * state + 8, 1)
        return jnp.where(slot8 == 2 * state, moved_re, moved_im)

    for n in range(5):
        grad_re, grad_im = summed(
            [[lines(coil, n * 10 + p) for p in range(10)] for coil in range(4)],
            [[maps(coil, z * 5 + n) for z in range(5)] for coil in range(4)],
            32,
            even32,
        )
        value = jnp.where(even32, over_groups(grad_re), over_groups(grad_im))
        for z in range(5):
            put(z * 5 + n, value[z * 32 : z * 32 + 32])
    grad_re, grad_im = summed(
        [[lines(coil, 50 + p) for p in range(10)] for coil in range(4)],
        [[maps(coil, 25 + z) for z in range(5)] for coil in range(4)],
        8,
        even8,
    )
    value = placed(in_group(grad_re), in_group(grad_im))
    for z in range(5):
        put(25 + z, value[z * 32 : z * 32 + 32])

    def across(rows):
        merged = None
        for coil, (row, source) in enumerate(rows):
            moved = moved_to(row, source, coil)
            merged = moved if merged is None else jnp.where(lane32 < 32 * coil, merged, moved)
        return merged

    grad_re, grad_im = summed(
        [[across([(lines(c, 60 + p // 4), p % 4) for c in range(4)]) for p in range(10)]],
        [[across([(maps(c, 30 + z // 4), z % 4) for c in range(4)]) for z in range(5)]],
        8,
        even8,
    )
    value = placed(in_group(over_groups(grad_re)), in_group(over_groups(grad_im)))
    merged = value[0:32]
    for z in range(1, 4):
        merged = jnp.where(lane32 < 32 * z, merged, value[z * 32 : z * 32 + 32])
    put(30, merged)
    put(31, value[128:160])

    if state == 1:
        row32 = lax.broadcasted_iota(jnp.int32, (32, 128), 0)
        first_state = jnp.where(row32 < 25, lane32 % 128, (lane32 % 32) * 4) < 64
        for q in range(32):
            both = jnp.where(
                first_state, before_ref[q * 32 : q * 32 + 32], t_ref[q * 32 : q * 32 + 32]
            ).astype(jnp.bfloat16)
            for copy in range(4):
                out_ref[q, copy] = both


def whole(array):
    return pl.BlockSpec(array.shape, lambda i: (0,) * len(array.shape))


def combine_coils(state, received, maps, table_z, before=()):
    scratch = [
        pltpu.VMEM((128 * 64, 128), jnp.float32),
        pltpu.VMEM((128 * 32, 128), jnp.float32),
    ]
    if state == 0:
        out_shape = jax.ShapeDtypeStruct((1024, 128), jnp.float32)
    else:
        out_shape = jax.ShapeDtypeStruct((32, 4, 32, 128), jnp.bfloat16)
        scratch.append(pltpu.VMEM((1024, 128), jnp.float32))
    return pl.pallas_call(
        functools.partial(combine_kernel, state),
        grid=(1,),
        in_specs=[whole(a) for a in (received, maps, table_z, *before)],
        out_specs=whole(out_shape),
        out_shape=out_shape,
        scratch_shapes=scratch,
        compiler_params=pltpu.CompilerParams(vmem_limit_bytes=SMALL_BYTES),
        cost_estimate=pl.CostEstimate(
            flops=3_000_000_000, bytes_accessed=20_000_000, transcendentals=0
        ),
        name="combine_coils",
    )(received, maps, table_z, *before)


def finish_kernel(g_ref, base_ref, out_ref, w_ref, x_ref, t_ref):
    def widen(i, carry):
        w_ref[pl.ds(i * 128, 128), :] = (
            g_ref[pl.ds(4 * i, 4)].reshape(128, 128).astype(jnp.float32)
        )
        return carry

    lax.fori_loop(0, 32, widen, 0)
    lane32 = lax.broadcasted_iota(jnp.int32, (32, 128), 1)
    lane40 = lax.broadcasted_iota(jnp.int32, (40, 128), 1)
    for z in range(5):
        for n in range(5):
            rest = None
            for quarter in range(4):
                x_ref[quarter, pl.ds(n, 32, stride=5), :] = w_ref[
                    pl.ds(quarter * 32 + z * 5 + n, 32, stride=128), :
                ]
                row, source = (25 + z, n) if n < 4 else (30 + z // 4, z % 4)
                moved = w_ref[pl.ds(quarter * 32 + row, 32, stride=128), :]
                shift = 32 * (quarter - source) % 128
                moved = pltpu.roll(moved, shift, 1) if shift else moved
                rest = moved if rest is None else jnp.where(lane32 < 32 * quarter, rest, moved)
            t_ref[pl.ds(n, 32, stride=5), :] = rest
        for group in range(4):
            state, part = group // 2, group % 2
            wide = [None] * 5

            def lay(value, source, lane, width):
                shift = (lane - source) % 128
                moved = pltpu.roll(value, shift, 1) if shift else value
                for b in range(lane // 128, (lane + width - 1) // 128 + 1):
                    old = wide[b]
                    wide[b] = (
                        moved if old is None else jnp.where(lane40 < lane - b * 128, old, moved)
                    )

            for i in range(4):
                rest = t_ref[pl.ds(i, 40, stride=4), :]
                for quarter in range(4):
                    start = i * 160 + quarter * 40
                    lay(x_ref[quarter, pl.ds(i, 40, stride=4), :], 32 * group, start, 32)
                    lay(rest, 32 * quarter + 8 * group, start + 32, 8)
            for b in range(5):
                at = pl.ds((state * 5 + z) * 400 + b * 2 + part, 40, stride=10)
                out_ref[at, :] = base_ref[at, :] - step_size * wide[b]


def finish(gathered, base):
    return pl.pallas_call(
        finish_kernel,
        grid=(1,),
        in_specs=[whole(gathered), whole(base)],
        out_specs=whole(base),
        out_shape=jax.ShapeDtypeStruct((4000, 128), jnp.float32),
        scratch_shapes=[
            pltpu.VMEM((128 * 32, 128), jnp.float32),
            pltpu.VMEM((4, 160, 128), jnp.float32),
            pltpu.VMEM((160, 128), jnp.float32),
        ],
        compiler_params=pltpu.CompilerParams(vmem_limit_bytes=SMALL_BYTES),
        cost_estimate=pl.CostEstimate(
            flops=10_000_000, bytes_accessed=6_000_000, transcendentals=0
        ),
        name="finish",
    )(gathered, base)


def tv_kernel(slab_ref, v_ref, low_ref, high_ref, out_ref, a_ref, fx_ref, fy_ref):
    shape = (200, 128)
    lane = lax.broadcasted_iota(jnp.int32, shape, 1)
    flat = lax.broadcasted_iota(jnp.int32, shape, 0) * 128 + lane
    y_pos = flat - IMG * ((flat * 52429) >> 23)
    y_ok = y_pos < IMG - 1
    x_ok = flat < IMG * (IMG - 1)
    has_low = jnp.where(slab_ref[0] > 0, 1.0, 0.0)
    has_high = jnp.where(slab_ref[0] < SLABS - 1, 1.0, 0.0)
    for ref in (a_ref, fx_ref, fy_ref):
        ref[...] = jnp.zeros((2, 216, 128), jnp.float32)

    def flow(delta_re, delta_im):
        inverse = lax.rsqrt(delta_re * delta_re + delta_im * delta_im + tv_smooth)
        return [delta_re * inverse, delta_im * inverse]

    def one_state(state, carry):
        sign = jnp.where(state == 0, -1.0, 1.0)

        def plane(which, z, part):
            return v_ref[pl.ds((which * 5 + z) * 400 + part, 200, stride=2), :]

        def edge(ref, part):
            return ref[pl.ds(state * 400 + part, 200, stride=2), :]

        here = [plane(state, 0, part) for part in range(2)]
        below = flow(*[(here[part] - edge(low_ref, part)) * has_low for part in range(2)])
        for z in range(5):
            if z < 4:
                after = [plane(state, z + 1, part) for part in range(2)]
                above = flow(*[after[part] - here[part] for part in range(2)])
            else:
                after = None
                above = flow(
                    *[(edge(high_ref, part) - here[part]) * has_high for part in range(2)]
                )
            between = flow(*[plane(1, z, part) - plane(0, z, part) for part in range(2)])
            total = [below[part] - above[part] + sign * between[part] for part in range(2)]
            delta_x, delta_y = [], []
            for part in range(2):
                a_ref[part, 8:208, :] = here[part]
                next1, next2 = a_ref[part, 9:209, :], a_ref[part, 10:210, :]
                y_next = jnp.where(
                    lane < 127, pltpu.roll(here[part], 127, 1), pltpu.roll(next1, 127, 1)
                )
                x_next = jnp.where(
                    lane < 96, pltpu.roll(next1, 96, 1), pltpu.roll(next2, 96, 1)
                )
                delta_y.append(jnp.where(y_ok, y_next - here[part], 0.0))
                delta_x.append(jnp.where(x_ok, x_next - here[part], 0.0))
            flow_x, flow_y = flow(*delta_x), flow(*delta_y)
            for part in range(2):
                fx_ref[part, 8:208, :] = flow_x[part]
                fy_ref[part, 8:208, :] = flow_y[part]
                before1, before2 = fx_ref[part, 7:207, :], fx_ref[part, 6:206, :]
                x_before = jnp.where(
                    lane >= 32, pltpu.roll(before1, 32, 1), pltpu.roll(before2, 32, 1)
                )
                before1 = fy_ref[part, 7:207, :]
                y_before = jnp.where(
                    lane >= 1, pltpu.roll(flow_y[part], 1, 1), pltpu.roll(before1, 1, 1)
                )
                grad = (
                    total[part] + (x_before - flow_x[part]) + (y_before - flow_y[part])
                )
                out_ref[pl.ds((state * 5 + z) * 400 + part, 200, stride=2), :] = here[
                    part
                ] - (step_size * tv_weight) * grad
            here, below = after, above
        return carry

    lax.fori_loop(0, 2, one_state, 0)


def tv_step(slab, image, low, high):
    spec = lambda array: pl.BlockSpec(array.shape, lambda i, *_: (0, 0))
    return pl.pallas_call(
        tv_kernel,
        grid_spec=pltpu.PrefetchScalarGridSpec(
            num_scalar_prefetch=1,
            grid=(1,),
            in_specs=[spec(image), spec(low), spec(high)],
            out_specs=spec(image),
            scratch_shapes=[pltpu.VMEM((2, 216, 128), jnp.float32) for _ in range(3)],
        ),
        out_shape=jax.ShapeDtypeStruct(image.shape, jnp.float32),
        compiler_params=pltpu.CompilerParams(vmem_limit_bytes=SMALL_BYTES),
        cost_estimate=pl.CostEstimate(
            flops=40_000_000, bytes_accessed=10_000_000, transcendentals=4_000_000
        ),
        name="tv_step",
    )(slab, image, low, high)


def flat_rows(volume):
    planes = volume.shape[2]
    rows = volume.reshape(2, 2, planes, 200, 128).transpose(0, 2, 3, 1, 4)
    return rows.reshape(planes * 800, 128)


def map_pieces(coil_maps):
    maps = coil_maps.reshape(2, 2, 5, 32, 5, 4, 40).transpose(3, 5, 2, 4, 0, 1, 6)
    main = maps[..., :32].reshape(128, 25, 128)
    rest = maps[..., 32:].reshape(128, 5, 5, 32)
    four = rest[:, :, :4].reshape(128, 5, 128)
    last = rest[:, :, 4].reshape(128, 160)
    last = jnp.pad(last, ((0, 0), (0, 96))).reshape(128, 2, 128)
    return jnp.concatenate([main, four, last], axis=1)


def per_device(
    image_now, coil_maps, kspace, row_offset, col_offset, tile_index, block_fill, slab_blocks
):
    states = 2
    planes_img = image_now.shape[2]
    img_len = IMG
    table_y, table_x, table_z = (jnp.asarray(t) for t in tables())
    everywhere = ("slab", "coil")

    maps_here = lax.all_to_all(map_pieces(coil_maps), everywhere, 0, 0, tiled=True)

    slot = jnp.arange(2048, dtype=jnp.int32)
    fill = jnp.where(slot[None, :] < slab_blocks, block_fill, 0)
    addr = (tile_index // 10) * 16 + tile_index % 10
    rows = row_offset.reshape(2, 1024, 128).transpose(1, 0, 2)
    cols = col_offset.reshape(2, 1024, 128).transpose(1, 0, 2)
    used = slab_blocks.reshape(2)
    received = []
    for state in range(states):
        lines = grid_lines(
            state, used, addr, fill, kspace, rows, cols, table_y, table_x
        )
        if state == 1:
            image_now, lines = lax.optimization_barrier((image_now, lines))
        received.append(
            lax.all_to_all(lines.reshape(128, 64, 128), everywhere, 0, 0, tiled=True)
        )
    shares = combine_coils(0, received[0], maps_here, table_z)
    shares = combine_coils(1, received[1], maps_here, table_z, (shares,))
    gathered = lax.all_to_all(shares.reshape(128, 32, 128), everywhere, 0, 0, tiled=True)
    pairs = [(i, i + 1) for i in range(SLABS - 1)]
    low = lax.ppermute(image_now[:, :, planes_img - 1 :], "slab", pairs)
    high = lax.ppermute(image_now[:, :, :1], "slab", [(j, i) for i, j in pairs])
    slab = lax.axis_index("slab").astype(jnp.int32).reshape(1)
    base = tv_step(slab, flat_rows(image_now), flat_rows(low), flat_rows(high))
    result = finish(gathered, base)
    result = result.reshape(states, planes_img, 200, 2, 128).transpose(0, 3, 1, 2, 4)
    return result.reshape(states, 2, planes_img, img_len * img_len)


def solution(mesh):
    return jax.shard_map(
        per_device,
        mesh=mesh,
        in_specs=(
            P(None, None, "slab", None),
            P("coil", None, "slab", None),
            P("coil", None, "slab", None),
            P(None, "slab"),
            P(None, "slab"),
            P(None, "slab"),
            P(None, "slab"),
            P(None, "slab"),
        ),
        out_specs=P(None, None, "slab", None),
        check_vma=False,
    )
```

```python
import functools
import math

import jax
import jax.numpy as jnp
import numpy as np
from jax import lax
from jax.experimental import pallas as pl
from jax.experimental.pallas import tpu as pltpu
from jax.sharding import PartitionSpec as P
import ml_dtypes

IMG = 160
TX = 4
TY = 32
BLK = 64
SLABS = 32

kernel_beta = 0.5
tv_smooth = 0.01
step_size = 0.5
tv_weight = 0.2

SCALE = math.sqrt(kernel_beta / math.log(2.0))
PLANES = 10
ROWS = 80
PAIRS_STEP = 32
VMEM_BYTES = 56 * 1024 * 1024
SMALL_BYTES = 32 * 1024 * 1024


def dft_parts():
    grid_len, img_len = 2 * IMG, IMG
    freq = np.arange(grid_len) - grid_len // 2
    pos = np.arange(img_len) - img_len // 2
    angles = np.mod(freq[:, None] * pos[None, :], grid_len).astype(np.float32)
    angles = angles * np.float32(2.0 * math.pi / grid_len)
    norm = np.float32(1.0 / math.sqrt(grid_len))
    return (np.cos(angles) * norm).astype(np.float32), (np.sin(angles) * norm).astype(np.float32)


def lane_of(coil, m):
    quarter, j = m // 40, m % 40
    pair, odd = quarter // 2, quarter % 2
    if j < 32:
        return pair * 128 + coil * 64 + odd * 32 + j
    return 256 + pair * 32 + coil * 16 + odd * 8 + (j - 32)


def tables():
    cosine, sine = dft_parts()
    table_y = np.zeros((2, 384, 2, 384), np.float32)
    for coil in range(2):
        for m in range(IMG):
            lane = lane_of(coil, m)
            table_y[coil, :320, 0, lane] = cosine[:, m]
            table_y[coil, :320, 1, lane] = sine[:, m]
    table_y = table_y.reshape(768, 768)
    cos_x = cosine.reshape(80, 4, 32, 5).transpose(3, 2, 0, 1)
    sin_x = sine.reshape(80, 4, 32, 5).transpose(3, 2, 0, 1)
    row_re = np.stack([cos_x, -sin_x], axis=3)
    row_im = np.stack([sin_x, cos_x], axis=3)
    table_x = np.stack([row_re, row_im]).reshape(320, 640)
    cos_z = cosine.reshape(32, 10, 32, 5).transpose(3, 2, 1, 0)
    sin_z = sine.reshape(32, 10, 32, 5).transpose(3, 2, 1, 0)
    table_z = np.stack([cos_z, sin_z]).reshape(320, 320)
    half = ml_dtypes.bfloat16
    return table_y.astype(half), table_x.astype(half), table_z.astype(half)


def grid_kernel(state, used_ref, addr_ref, fill_ref, ks_ref, row_ref, col_ref, *refs):
    maps_ref, refs = (refs[0], refs[1:]) if state == 0 else (None, refs)
    ty_ref, tx_ref, out_ref, g_ref, o_ref, p_ref, q_ref, s_ref, t_ref = refs
    lane = lax.broadcasted_iota(jnp.int32, (8, 128), 1)
    sub = lax.broadcasted_iota(jnp.int32, (8, 128), 0)
    left = lane < 64
    upper = sub < 4
    left_row = lax.broadcasted_iota(jnp.int32, (1, 128), 1) < 64
    col_pos = lax.broadcasted_iota(jnp.int32, (32, 128), 0).astype(jnp.float32) * SCALE
    row_pos = (sub & 3).astype(jnp.float32) * SCALE
    zero = jnp.zeros((8, 128), jnp.float32)

    def clear(i, carry):
        g_ref[pl.ds(i * 8, 8)] = jnp.zeros((8, 3, 2, 8, 128), jnp.float32)
        return carry

    lax.fori_loop(0, PLANES * ROWS // 8, clear, 0)

    def add_pair(done, p):
        first = jnp.maximum(done, 0) * (2 * PAIRS_STEP) + 2 * p
        for which in range(2):
            addr = addr_ref[state, first + which]
            g_ref[addr >> 4, (addr >> 2) & 3] += o_ref[done & 1, p, which]

    def step(it, carry):
        base = it * (2 * PAIRS_STEP)
        re_rows, im_rows = [], []
        for coil in range(2):
            even = ks_ref[coil, 0, pl.ds(base, PAIRS_STEP, stride=2), :]
            odd = ks_ref[coil, 0, pl.ds(base + 1, PAIRS_STEP, stride=2), :]
            re_rows.append(jnp.where(left_row, even, pltpu.roll(odd, 64, 1)))
            im_rows.append(jnp.where(left_row, pltpu.roll(even, 64, 1), odd))
        for p in range(PAIRS_STEP):
            add_pair(it - 1, p)
            pair = it * PAIRS_STEP + p
            col = col_ref[pair][state : state + 1] * SCALE
            row = row_ref[pair][state : state + 1] * SCALE
            diff_y = col_pos - col
            weight_y = jnp.exp2(-(diff_y * diff_y)).astype(jnp.bfloat16)
            addr0 = addr_ref[state, base + 2 * p]
            addr1 = addr_ref[state, base + 2 * p + 1]
            spot = jnp.where(left_row, addr0 & 3, addr1 & 3)
            placed = jnp.concatenate(
                [weight_y * jnp.where(spot == b, 1.0, 0.0).astype(jnp.bfloat16) for b in range(4)],
                axis=0,
            )
            limit = jnp.where(
                left, fill_ref[state, base + 2 * p], fill_ref[state, base + 2 * p + 1] + 64
            )
            diff_x = row_pos - row
            weight_x = jnp.where(lane < limit, jnp.exp2(-(diff_x * diff_x)), 0.0)
            parts = [
                jnp.where(
                    upper,
                    jnp.broadcast_to(re_rows[coil][p : p + 1], (8, 128)),
                    jnp.broadcast_to(im_rows[coil][p : p + 1], (8, 128)),
                )
                * weight_x
                for coil in range(2)
            ]
            samples = jnp.concatenate(
                [jnp.where(left, part, zero) for part in parts]
                + [jnp.where(left, zero, part) for part in parts],
                axis=0,
            ).astype(jnp.bfloat16)
            o_ref[it & 1, p] = lax.dot_general(
                samples, placed, (((1,), (1,)), ((), ())), preferred_element_type=jnp.float32
            ).reshape(2, 2, 8, 128)
        return carry

    steps = (used_ref[state] + 2 * PAIRS_STEP - 1) // (2 * PAIRS_STEP)
    o_ref[1] = jnp.zeros((PAIRS_STEP, 2, 2, 8, 128), jnp.float32)
    lax.fori_loop(0, steps, step, 0)
    for p in range(PAIRS_STEP):
        add_pair(steps - 1, p)

    lane32 = lax.broadcasted_iota(jnp.int32, (32, 128), 1)
    even32 = (lane32 // 32) % 2 == 0
    even8 = (lane32 // 8) % 2 == 0

    def one_plane(plane, carry):
        lines = jnp.concatenate(
            [
                g_ref[pl.ds(plane * ROWS, ROWS), quad, coil].reshape(640, 128).astype(jnp.bfloat16)
                for coil in range(2)
                for quad in range(3)
            ],
            axis=1,
        )
        p_ref[...] = jnp.dot(lines, ty_ref[...], preferred_element_type=jnp.float32).astype(
            jnp.bfloat16
        )
        q_ref[...] = jnp.dot(tx_ref[...], p_ref[...], preferred_element_type=jnp.float32)
        merged = [None] * 4
        for n in range(5):
            lo, hi = n * 32, 160 + n * 32
            re_part = q_ref[lo : lo + 32, 0:384] - q_ref[hi : hi + 32, 384:768]
            im_part = q_ref[hi : hi + 32, 0:384] + q_ref[lo : lo + 32, 384:768]
            for pair in range(2):
                re_e = re_part[:, pair * 128 : pair * 128 + 128]
                im_e = im_part[:, pair * 128 : pair * 128 + 128]
                at = pl.ds(n * 10 + plane, 32, stride=64)
                s_ref[2 * pair, at, :] = jnp.where(even32, re_e, pltpu.roll(im_e, 32, 1))
                s_ref[2 * pair + 1, at, :] = jnp.where(even32, pltpu.roll(re_e, 96, 1), im_e)
            re_t, im_t = re_part[:, 256:384], im_part[:, 256:384]
            rest = (
                jnp.where(even8, re_t, pltpu.roll(im_t, 8, 1)),
                jnp.where(even8, pltpu.roll(re_t, 120, 1), im_t),
            )
            if n == 4:
                for odd in range(2):
                    t_ref[plane, odd] = rest[odd]
                continue
            for quarter in range(4):
                shift = 32 * (n - quarter // 2) % 128
                moved = pltpu.roll(rest[quarter % 2], shift, 1) if shift else rest[quarter % 2]
                before = merged[quarter]
                merged[quarter] = (
                    moved if before is None else jnp.where(lane32 < 32 * n, before, moved)
                )
        for quarter in range(4):
            s_ref[quarter, pl.ds(50 + plane, 32, stride=64), :] = merged[quarter]
        return carry

    lax.fori_loop(0, PLANES, one_plane, 0)
    for quarter in range(4):
        for group in range(3):
            merged = None
            for v in range(4 if group < 2 else 2):
                shift = 32 * (v - quarter // 2) % 128
                moved = t_ref[4 * group + v, quarter % 2]
                moved = pltpu.roll(moved, shift, 1) if shift else moved
                merged = moved if merged is None else jnp.where(lane32 < 32 * v, merged, moved)
            s_ref[quarter, pl.ds(60 + group, 32, stride=64), :] = merged
        for q in range(32):
            out_ref[q, quarter, 0:64] = s_ref[quarter, q * 64 : q * 64 + 64, :].astype(jnp.bfloat16)
            if state == 0:
                out_ref[q, quarter, 64:96] = maps_ref[4 * q + quarter]


def grid_lines(state, used, addr, fill, kspace, rows, cols, extra, table_y, table_x):
    out_rows = 64 if state else 96
    return pl.pallas_call(
        functools.partial(grid_kernel, state),
        grid_spec=pltpu.PrefetchScalarGridSpec(
            num_scalar_prefetch=3,
            grid=(1,),
            in_specs=[
                pl.BlockSpec((2, 1, 2048, 128), lambda i, *_: (0, state, 0, 0)),
                pl.BlockSpec((1024, 2, 128), lambda i, *_: (0, 0, 0)),
                pl.BlockSpec((1024, 2, 128), lambda i, *_: (0, 0, 0)),
                *[pl.BlockSpec(e.shape, lambda i, *_: (0, 0, 0)) for e in extra],
                pl.BlockSpec((768, 768), lambda i, *_: (0, 0)),
                pl.BlockSpec((320, 640), lambda i, *_: (0, 0)),
            ],
            out_specs=pl.BlockSpec((32, 4, out_rows, 128), lambda i, *_: (0, 0, 0, 0)),
            scratch_shapes=[
                pltpu.VMEM((PLANES * ROWS, 3, 2, 8, 128), jnp.float32),
                pltpu.VMEM((2, PAIRS_STEP, 2, 2, 8, 128), jnp.float32),
                pltpu.VMEM((640, 768), jnp.bfloat16),
                pltpu.VMEM((320, 768), jnp.float32),
                pltpu.VMEM((4, 32 * 64, 128), jnp.float32),
                pltpu.VMEM((PLANES, 2, 32, 128), jnp.float32),
            ],
        ),
        out_shape=jax.ShapeDtypeStruct((32, 4, out_rows, 128), jnp.bfloat16),
        compiler_params=pltpu.CompilerParams(vmem_limit_bytes=VMEM_BYTES),
        cost_estimate=pl.CostEstimate(
            flops=20_000_000_000, bytes_accessed=100_000_000, transcendentals=10_000_000
        ),
        name="grid_lines",
    )(used, addr, fill, kspace, rows, cols, *extra, table_y, table_x)


def swap_parts(value, group, even):
    return jnp.where(even, pltpu.roll(value, 128 - group, 1), -pltpu.roll(value, group, 1))


def combine_kernel(state, *refs):
    if state == 0:
        x_ref, maps_ref, tz_ref, out_ref, f_ref, m_ref = refs
        t_ref = out_ref
    else:
        x_ref, maps_ref, tz_ref, before_ref, out_ref, f_ref, m_ref, t_ref = refs

    def widen(i, carry):
        f_ref[pl.ds(i * 128, 128), :] = (
            x_ref[pl.ds(2 * i, 2)].reshape(128, 128).astype(jnp.float32)
        )
        m_ref[pl.ds(i * 64, 64), :] = (
            maps_ref[pl.ds(2 * i, 2)].reshape(64, 128).astype(jnp.float32)
        )
        return carry

    lax.fori_loop(0, 64, widen, 0)

    lane = lax.broadcasted_iota(jnp.int32, (160, 128), 1)
    lane32 = lax.broadcasted_iota(jnp.int32, (32, 128), 1)
    even32 = (lane // 32) % 2 == 0
    even8 = (lane // 8) % 2 == 0
    slot8 = (lane // 8) % 4
    zero = jnp.zeros((160, 128), jnp.float32)

    def lines(coil, row):
        return f_ref[pl.ds(coil * 64 + row, 32, stride=256), :]

    def maps(coil, row):
        return m_ref[pl.ds(coil * 32 + row, 32, stride=128), :]

    def moved_to(value, source, target):
        shift = 32 * (target - source) % 128
        return pltpu.roll(value, shift, 1) if shift else value

    def summed(line_rows, map_rows, group, even):
        grad_re, grad_im = zero, zero
        for first in range(0, len(line_rows), 2):
            block = line_rows[first : first + 2]
            spread = jnp.concatenate(
                [jnp.concatenate(r, axis=0).astype(jnp.bfloat16) for r in block], axis=1
            )
            image = jnp.dot(tz_ref[...], spread, preferred_element_type=jnp.float32)
            for k in range(len(block)):
                by_cos = image[:160, k * 128 : k * 128 + 128]
                by_sin = image[160:, k * 128 : k * 128 + 128]
                here = jnp.concatenate(map_rows[first + k], axis=0)
                swapped = swap_parts(here, group, even)
                grad_re = grad_re + by_cos * here + by_sin * swapped
                grad_im = grad_im + by_sin * here - by_cos * swapped
        return grad_re, grad_im

    def put(row, value):
        t_ref[pl.ds(row, 32, stride=32), :] = value

    def over_groups(value):
        value = value + pltpu.roll(value, 64, 1)
        return value + pltpu.roll(value, 32, 1)

    def in_group(value):
        value = value + pltpu.roll(value, 112, 1)
        return value + pltpu.roll(value, 120, 1)

    def placed(grad_re, grad_im):
        moved_re = pltpu.roll(grad_re, 16, 1) if state else grad_re
        moved_im = pltpu.roll(grad_im, 16 * state + 8, 1)
        return jnp.where(slot8 == 2 * state, moved_re, moved_im)

    for n in range(5):
        grad_re, grad_im = summed(
            [[lines(coil, n * 10 + p) for p in range(10)] for coil in range(4)],
            [[maps(coil, z * 5 + n) for z in range(5)] for coil in range(4)],
            32,
            even32,
        )
        value = jnp.where(even32, over_groups(grad_re), over_groups(grad_im))
        for z in range(5):
            put(z * 5 + n, value[z * 32 : z * 32 + 32])
    grad_re, grad_im = summed(
        [[lines(coil, 50 + p) for p in range(10)] for coil in range(4)],
        [[maps(coil, 25 + z) for z in range(5)] for coil in range(4)],
        8,
        even8,
    )
    value = placed(in_group(grad_re), in_group(grad_im))
    for z in range(5):
        put(25 + z, value[z * 32 : z * 32 + 32])

    def across(rows):
        merged = None
        for coil, (row, source) in enumerate(rows):
            moved = moved_to(row, source, coil)
            merged = moved if merged is None else jnp.where(lane32 < 32 * coil, merged, moved)
        return merged

    grad_re, grad_im = summed(
        [[across([(lines(c, 60 + p // 4), p % 4) for c in range(4)]) for p in range(10)]],
        [[across([(maps(c, 30 + z // 4), z % 4) for c in range(4)]) for z in range(5)]],
        8,
        even8,
    )
    value = placed(in_group(over_groups(grad_re)), in_group(over_groups(grad_im)))
    merged = value[0:32]
    for z in range(1, 4):
        merged = jnp.where(lane32 < 32 * z, merged, value[z * 32 : z * 32 + 32])
    put(30, merged)
    put(31, value[128:160])

    if state == 1:
        row32 = lax.broadcasted_iota(jnp.int32, (32, 128), 0)
        first_state = jnp.where(row32 < 25, lane32 % 128, (lane32 % 32) * 4) < 64
        for q in range(32):
            both = jnp.where(
                first_state, before_ref[q * 32 : q * 32 + 32], t_ref[q * 32 : q * 32 + 32]
            ).astype(jnp.bfloat16)
            for copy in range(4):
                out_ref[q, copy] = both


def whole(array):
    return pl.BlockSpec(array.shape, lambda i: (0,) * len(array.shape))


def combine_coils(state, received, maps, table_z, before=()):
    scratch = [
        pltpu.VMEM((128 * 64, 128), jnp.float32),
        pltpu.VMEM((128 * 32, 128), jnp.float32),
    ]
    if state == 0:
        out_shape = jax.ShapeDtypeStruct((1024, 128), jnp.float32)
    else:
        out_shape = jax.ShapeDtypeStruct((32, 4, 32, 128), jnp.bfloat16)
        scratch.append(pltpu.VMEM((1024, 128), jnp.float32))
    return pl.pallas_call(
        functools.partial(combine_kernel, state),
        grid=(1,),
        in_specs=[
            pl.BlockSpec((128, 64, 128), lambda i: (0, 0, 0)),
            pl.BlockSpec((128, 32, 128), lambda i: (0, 2, 0)),
            whole(table_z),
            *[whole(b) for b in before],
        ],
        out_specs=whole(out_shape),
        out_shape=out_shape,
        scratch_shapes=scratch,
        compiler_params=pltpu.CompilerParams(vmem_limit_bytes=SMALL_BYTES),
        cost_estimate=pl.CostEstimate(
            flops=3_000_000_000, bytes_accessed=20_000_000, transcendentals=0
        ),
        name="combine_coils",
    )(received, maps, table_z, *before)


def finish_kernel(g_ref, base_ref, out_ref, w_ref, x_ref, t_ref):
    def widen(i, carry):
        w_ref[pl.ds(i * 128, 128), :] = (
            g_ref[pl.ds(4 * i, 4)].reshape(128, 128).astype(jnp.float32)
        )
        return carry

    lax.fori_loop(0, 32, widen, 0)
    lane32 = lax.broadcasted_iota(jnp.int32, (32, 128), 1)
    lane40 = lax.broadcasted_iota(jnp.int32, (40, 128), 1)
    for z in range(5):
        for n in range(5):
            rest = None
            for quarter in range(4):
                x_ref[quarter, pl.ds(n, 32, stride=5), :] = w_ref[
                    pl.ds(quarter * 32 + z * 5 + n, 32, stride=128), :
                ]
                row, source = (25 + z, n) if n < 4 else (30 + z // 4, z % 4)
                moved = w_ref[pl.ds(quarter * 32 + row, 32, stride=128), :]
                shift = 32 * (quarter - source) % 128
                moved = pltpu.roll(moved, shift, 1) if shift else moved
                rest = moved if rest is None else jnp.where(lane32 < 32 * quarter, rest, moved)
            t_ref[pl.ds(n, 32, stride=5), :] = rest
        for group in range(4):
            state, part = group // 2, group % 2
            wide = [None] * 5

            def lay(value, source, lane, width):
                shift = (lane - source) % 128
                moved = pltpu.roll(value, shift, 1) if shift else value
                for b in range(lane // 128, (lane + width - 1) // 128 + 1):
                    old = wide[b]
                    wide[b] = (
                        moved if old is None else jnp.where(lane40 < lane - b * 128, old, moved)
                    )

            for i in range(4):
                rest = t_ref[pl.ds(i, 40, stride=4), :]
                for quarter in range(4):
                    start = i * 160 + quarter * 40
                    lay(x_ref[quarter, pl.ds(i, 40, stride=4), :], 32 * group, start, 32)
                    lay(rest, 32 * quarter + 8 * group, start + 32, 8)
            for b in range(5):
                at = pl.ds((state * 5 + z) * 400 + b * 2 + part, 40, stride=10)
                out_ref[at, :] = base_ref[at, :] - step_size * wide[b]


def finish(gathered, base):
    return pl.pallas_call(
        finish_kernel,
        grid=(1,),
        in_specs=[whole(gathered), whole(base)],
        out_specs=whole(base),
        out_shape=jax.ShapeDtypeStruct((4000, 128), jnp.float32),
        scratch_shapes=[
            pltpu.VMEM((128 * 32, 128), jnp.float32),
            pltpu.VMEM((4, 160, 128), jnp.float32),
            pltpu.VMEM((160, 128), jnp.float32),
        ],
        compiler_params=pltpu.CompilerParams(vmem_limit_bytes=SMALL_BYTES),
        cost_estimate=pl.CostEstimate(
            flops=10_000_000, bytes_accessed=6_000_000, transcendentals=0
        ),
        name="finish",
    )(gathered, base)


def tv_kernel(slab_ref, v_ref, low_ref, high_ref, out_ref, a_ref, fx_ref, fy_ref):
    shape = (200, 128)
    lane = lax.broadcasted_iota(jnp.int32, shape, 1)
    flat = lax.broadcasted_iota(jnp.int32, shape, 0) * 128 + lane
    y_pos = flat - IMG * ((flat * 52429) >> 23)
    y_ok = y_pos < IMG - 1
    x_ok = flat < IMG * (IMG - 1)
    has_low = jnp.where(slab_ref[0] > 0, 1.0, 0.0)
    has_high = jnp.where(slab_ref[0] < SLABS - 1, 1.0, 0.0)
    for ref in (a_ref, fx_ref, fy_ref):
        ref[...] = jnp.zeros((2, 216, 128), jnp.float32)

    def flow(delta_re, delta_im):
        inverse = lax.rsqrt(delta_re * delta_re + delta_im * delta_im + tv_smooth)
        return [delta_re * inverse, delta_im * inverse]

    def one_state(state, carry):
        sign = jnp.where(state == 0, -1.0, 1.0)

        def plane(which, z, part):
            return v_ref[pl.ds((which * 5 + z) * 400 + part, 200, stride=2), :]

        def edge(ref, part):
            return ref[pl.ds(state * 400 + part, 200, stride=2), :]

        here = [plane(state, 0, part) for part in range(2)]
        below = flow(*[(here[part] - edge(low_ref, part)) * has_low for part in range(2)])
        for z in range(5):
            if z < 4:
                after = [plane(state, z + 1, part) for part in range(2)]
                above = flow(*[after[part] - here[part] for part in range(2)])
            else:
                after = None
                above = flow(
                    *[(edge(high_ref, part) - here[part]) * has_high for part in range(2)]
                )
            between = flow(*[plane(1, z, part) - plane(0, z, part) for part in range(2)])
            total = [below[part] - above[part] + sign * between[part] for part in range(2)]
            delta_x, delta_y = [], []
            for part in range(2):
                a_ref[part, 8:208, :] = here[part]
                next1, next2 = a_ref[part, 9:209, :], a_ref[part, 10:210, :]
                y_next = jnp.where(
                    lane < 127, pltpu.roll(here[part], 127, 1), pltpu.roll(next1, 127, 1)
                )
                x_next = jnp.where(
                    lane < 96, pltpu.roll(next1, 96, 1), pltpu.roll(next2, 96, 1)
                )
                delta_y.append(jnp.where(y_ok, y_next - here[part], 0.0))
                delta_x.append(jnp.where(x_ok, x_next - here[part], 0.0))
            flow_x, flow_y = flow(*delta_x), flow(*delta_y)
            for part in range(2):
                fx_ref[part, 8:208, :] = flow_x[part]
                fy_ref[part, 8:208, :] = flow_y[part]
                before1, before2 = fx_ref[part, 7:207, :], fx_ref[part, 6:206, :]
                x_before = jnp.where(
                    lane >= 32, pltpu.roll(before1, 32, 1), pltpu.roll(before2, 32, 1)
                )
                before1 = fy_ref[part, 7:207, :]
                y_before = jnp.where(
                    lane >= 1, pltpu.roll(flow_y[part], 1, 1), pltpu.roll(before1, 1, 1)
                )
                grad = (
                    total[part] + (x_before - flow_x[part]) + (y_before - flow_y[part])
                )
                out_ref[pl.ds((state * 5 + z) * 400 + part, 200, stride=2), :] = here[
                    part
                ] - (step_size * tv_weight) * grad
            here, below = after, above
        return carry

    lax.fori_loop(0, 2, one_state, 0)


def tv_step(slab, image, low, high):
    spec = lambda array: pl.BlockSpec(array.shape, lambda i, *_: (0, 0))
    return pl.pallas_call(
        tv_kernel,
        grid_spec=pltpu.PrefetchScalarGridSpec(
            num_scalar_prefetch=1,
            grid=(1,),
            in_specs=[spec(image), spec(low), spec(high)],
            out_specs=spec(image),
            scratch_shapes=[pltpu.VMEM((2, 216, 128), jnp.float32) for _ in range(3)],
        ),
        out_shape=jax.ShapeDtypeStruct(image.shape, jnp.float32),
        compiler_params=pltpu.CompilerParams(vmem_limit_bytes=SMALL_BYTES),
        cost_estimate=pl.CostEstimate(
            flops=40_000_000, bytes_accessed=10_000_000, transcendentals=4_000_000
        ),
        name="tv_step",
    )(slab, image, low, high)


def flat_rows(volume):
    planes = volume.shape[2]
    rows = volume.reshape(2, 2, planes, 200, 128).transpose(0, 2, 3, 1, 4)
    return rows.reshape(planes * 800, 128)


def map_kernel(maps_ref, out_ref, v_ref, w_ref, x_ref, t_ref, last_ref):
    def widen(i, carry):
        at = pl.ds(i * 160, 160)
        v_ref[at, :] = maps_ref[at, :].astype(jnp.float32)
        return carry

    lax.fori_loop(0, 25, widen, 0)
    lane32 = lax.broadcasted_iota(jnp.int32, (32, 128), 1)
    lane40 = lax.broadcasted_iota(jnp.int32, (40, 128), 1)

    def turned(value, shift):
        return pltpu.roll(value, shift % 128, 1) if shift % 128 else value

    for z in range(5):
        for i in range(4):
            rest = None
            for quarter in range(4):
                start = i * 160 + quarter * 40
                main = None
                for group in range(4):
                    coil, part = group // 2, group % 2

                    def piece(lane, target, width):
                        b, inside = lane // 128, lane % 128
                        at = (coil * 5 + z) * 400 + part
                        value = turned(
                            v_ref[pl.ds(at + 2 * b, 40, stride=10), :], target - inside
                        )
                        if inside + width > 128:
                            follow = turned(
                                v_ref[pl.ds(at + 2 * b + 2, 40, stride=10), :], target - inside
                            )
                            value = jnp.where(lane40 < target + 128 - inside, value, follow)
                        return value

                    value = piece(start, 32 * group, 32)
                    main = value if main is None else jnp.where(lane40 < 32 * group, main, value)
                    target = 32 * quarter + 8 * group
                    value = piece(start + 32, target, 8)
                    rest = value if rest is None else jnp.where(lane40 < target, rest, value)
                x_ref[quarter, pl.ds(i, 40, stride=4), :] = main
            t_ref[pl.ds(i, 40, stride=4), :] = rest
        for n in range(5):
            for quarter in range(4):
                w_ref[pl.ds(quarter * 32 + z * 5 + n, 32, stride=128), :] = x_ref[
                    quarter, pl.ds(n, 32, stride=5), :
                ]
        tails = [t_ref[pl.ds(n, 32, stride=5), :] for n in range(5)]
        last_ref[z] = tails[4]
        for quarter in range(4):
            merged = turned(tails[0], -32 * quarter)
            for n in range(1, 4):
                merged = jnp.where(lane32 < 32 * n, merged, turned(tails[n], 32 * (n - quarter)))
            w_ref[pl.ds(quarter * 32 + 25 + z, 32, stride=128), :] = merged
    for quarter in range(4):
        merged = turned(last_ref[0], -32 * quarter)
        for z in range(1, 4):
            merged = jnp.where(
                lane32 < 32 * z, merged, turned(last_ref[z], 32 * (z - quarter))
            )
        w_ref[pl.ds(quarter * 32 + 30, 32, stride=128), :] = merged
        w_ref[pl.ds(quarter * 32 + 31, 32, stride=128), :] = turned(
            last_ref[4], -32 * quarter
        )

    def narrow(i, carry):
        out_ref[pl.ds(4 * i, 4)] = (
            w_ref[pl.ds(i * 128, 128), :].reshape(4, 32, 128).astype(jnp.bfloat16)
        )
        return carry

    lax.fori_loop(0, 32, narrow, 0)


def map_pieces(coil_maps):
    rows = flat_rows(coil_maps)
    out_shape = jax.ShapeDtypeStruct((128, 32, 128), jnp.bfloat16)
    return pl.pallas_call(
        map_kernel,
        grid=(1,),
        in_specs=[whole(rows)],
        out_specs=whole(out_shape),
        out_shape=out_shape,
        scratch_shapes=[
            pltpu.VMEM((4000, 128), jnp.float32),
            pltpu.VMEM((128 * 32, 128), jnp.float32),
            pltpu.VMEM((4, 160, 128), jnp.float32),
            pltpu.VMEM((160, 128), jnp.float32),
            pltpu.VMEM((5, 32, 128), jnp.float32),
        ],
        compiler_params=pltpu.CompilerParams(vmem_limit_bytes=SMALL_BYTES),
        cost_estimate=pl.CostEstimate(flops=10_000_000, bytes_accessed=6_000_000, transcendentals=0),
        name="map_pieces",
    )(rows)


def per_device(
    image_now, coil_maps, kspace, row_offset, col_offset, tile_index, block_fill, slab_blocks
):
    states = 2
    planes_img = image_now.shape[2]
    img_len = IMG
    table_y, table_x, table_z = (jnp.asarray(t) for t in tables())
    everywhere = ("slab", "coil")

    slot = jnp.arange(2048, dtype=jnp.int32)
    fill = jnp.where(slot[None, :] < slab_blocks, block_fill, 0)
    addr = (tile_index // 10) * 16 + tile_index % 10
    rows = row_offset.reshape(2, 1024, 128).transpose(1, 0, 2)
    cols = col_offset.reshape(2, 1024, 128).transpose(1, 0, 2)
    used = slab_blocks.reshape(2)
    received = []
    for state in range(states):
        extra = () if state else (map_pieces(coil_maps),)
        lines = grid_lines(
            state, used, addr, fill, kspace, rows, cols, extra, table_y, table_x
        )
        if state == 0:
            used, lines = lax.optimization_barrier((used, lines))
        else:
            image_now, lines, received[0] = lax.optimization_barrier(
                (image_now, lines, received[0])
            )
        lines = lines.reshape(128, lines.shape[2], 128)
        received.append(lax.all_to_all(lines, everywhere, 0, 0, tiled=True))
    pairs = [(i, i + 1) for i in range(SLABS - 1)]
    low = lax.ppermute(image_now[:, :, planes_img - 1 :], "slab", pairs)
    high = lax.ppermute(image_now[:, :, :1], "slab", [(j, i) for i, j in pairs])
    slab = lax.axis_index("slab").astype(jnp.int32).reshape(1)
    base = tv_step(slab, flat_rows(image_now), flat_rows(low), flat_rows(high))

    shares = combine_coils(0, received[0], received[0], table_z)
    last, base = lax.optimization_barrier((received[1], base))
    shares = combine_coils(1, last, received[0], table_z, (shares,))
    gathered = lax.all_to_all(shares.reshape(128, 32, 128), everywhere, 0, 0, tiled=True)
    result = finish(gathered, base)
    result = result.reshape(states, planes_img, 200, 2, 128).transpose(0, 3, 1, 2, 4)
    return result.reshape(states, 2, planes_img, img_len * img_len)


def solution(mesh):
    return jax.shard_map(
        per_device,
        mesh=mesh,
        in_specs=(
            P(None, None, "slab", None),
            P("coil", None, "slab", None),
            P("coil", None, "slab", None),
            P(None, "slab"),
            P(None, "slab"),
            P(None, "slab"),
            P(None, "slab"),
            P(None, "slab"),
        ),
        out_specs=P(None, None, "slab", None),
        check_vma=False,
    )
```
